32 devices in a mesh: req: 8 (over z, y), mlp: 4 (over x, core).
Axes of the slice: x: 2, y: 2, z: 4, core: 2. Of those that a mesh axis runs over, the one named last changes fastest.
Arguments:
- residual: bfloat16 [2048, 2048], P('req'), may hold values from -20 to 20
- query_rows: bfloat16 [2048, 2048], P('req', 'mlp'), may hold values from -6 to 6
- value_rows: bfloat16 [2048, 2048], P('req', 'mlp'), may hold values from -6 to 6
- forget_logit: float32 [2048, 2048], P('req', 'mlp'), may hold values from 0 to 40
- slot_kind: int32 [2048], P('req'), may hold values from 0 to 2, as said below
- head_gain: float32 [2048], P('mlp'), may hold values from 0.1 to 1.9
- out_weight: bfloat16 [2048, 2048], P('mlp', 'req'), may hold values from -0.125 to 0.125
- ffn_gain: float32 [2048], replicated, may hold values from 0.1 to 1.9
- gate_weight: bfloat16 [2048, 3072], P('req', 'mlp'), may hold values from -0.125 to 0.125
- up_weight: bfloat16 [2048, 3072], P('req', 'mlp'), may hold values from -0.125 to 0.125
- down_weight: bfloat16 [3072, 2048], P('mlp', 'req'), may hold values from -0.109375 to 0.109375
Outputs:
- layer_out: bfloat16 [2048, 2048], P('req', 'mlp')
The draws below stay inside these ranges and needn't reach their ends.
Inputs may be any that keep to these rules, and one draw needn't show every extreme that they name: `slot_kind`: slots 0 to 1535 hold one prompt: slot 0 has kind 2, the others kind 1. Every other block of 256 slots holds short requests packed from its first slot, then empty slots; a short request has at most 32 tokens, the first request of each such block exactly 32. Over all 2048 slots exactly 1664 are live.
All inputs are finite; a program needn't handle non-finite values.
Results may differ from the reference program's by a relative error of at most 0.0163.
Values may be sent and summed in bfloat16 or wider, within the bound.
A program may use at most 128 MiB of HBM per device.

```python
import jax
import jax.numpy as jnp
from jax import lax

MODEL_WIDTH = 2048
HEADS = 16
HEAD = 128
FF = 3072
SPAN = 32
SHORT_MAX = 32
SLOTS = 256
TOKEN_SLOTS = 2048
LONG = 1536
N_MLP = 4


def draw_slot_kind(key, part):
    key_len = jax.random.fold_in(key, 11)
    key_cut = jax.random.fold_in(key, 12)
    slot_numbers = jnp.arange(TOKEN_SLOTS)
    inside = slot_numbers % SLOTS
    pair_count = max((TOKEN_SLOTS - LONG) // (2 * SLOTS), 1)
    shifts = jax.random.randint(key_len, (pair_count,), 0, SLOTS // 8 + 1)
    short_dev = jnp.maximum(slot_numbers - LONG, 0) // SLOTS
    pair_id = jnp.minimum(short_dev // 2, pair_count - 1)
    sign_val = 1 - 2 * (short_dev % 2)
    length = SLOTS // 4 + sign_val * shifts[pair_id]
    live_short = inside < length
    random_cut = jax.random.randint(key_cut, (TOKEN_SLOTS,), 0, 12) == 0
    cut_here = (inside == 0) | (inside == SHORT_MAX) | (inside > SHORT_MAX) & ((inside % SHORT_MAX == 0) | random_cut)
    short_kind = jnp.where(live_short, jnp.where(cut_here, 2, 1), 0)
    long_kind = jnp.where(slot_numbers == 0, 2, 1)
    return jnp.where(slot_numbers < LONG, long_kind, short_kind).astype(jnp.int32)


def draw_forget_logit(key, part):
    key_rows = [jax.random.fold_in(key, 21 + index) for index in range(6)]
    heads_all = MODEL_WIDTH // HEAD
    slow_share = 0.5
    head_slow = jax.random.uniform(key_rows[0], (heads_all,)) < slow_share
    channel_slow = head_slow[jnp.arange(MODEL_WIDTH) // HEAD]
    spread = jax.random.uniform(key_rows[1], (MODEL_WIDTH,))
    rate_slow = jnp.exp(jnp.log(0.2 / LONG) + spread * jnp.log(5.0))
    rate_fast = jnp.exp(jnp.log(1.0 / 400.0) + spread * jnp.log(400.0 / 25.0))
    base_rate = jnp.where(channel_slow, rate_slow, rate_fast)
    slot_numbers = jnp.arange(TOKEN_SLOTS)
    device_factor = jnp.exp(jax.random.uniform(key_rows[2], (TOKEN_SLOTS // SLOTS, MODEL_WIDTH), minval=-0.7, maxval=0.7))
    token_factor = jnp.exp(jax.random.uniform(key_rows[3], (TOKEN_SLOTS, MODEL_WIDTH), minval=-0.3, maxval=0.3))
    decay_speed = jnp.minimum(base_rate[None] * device_factor[slot_numbers // SLOTS] * token_factor, 0.1)
    spike_rows = jax.random.randint(key_rows[4], (8,), 0, TOKEN_SLOTS)
    spike_flags = jnp.any(slot_numbers[:, None] == spike_rows[None, :], axis=1)
    spike_rate = jax.random.uniform(key_rows[5], (TOKEN_SLOTS, MODEL_WIDTH), minval=0.2, maxval=0.5)
    decay_speed = jnp.where(spike_flags[:, None], spike_rate, decay_speed)
    return (jnp.log1p(-decay_speed) - jnp.log(decay_speed)).astype(jnp.float32)


def draw_residual(key, part):
    key_val = jax.random.fold_in(key, 31)
    key_row = jax.random.fold_in(key, 32)
    row_scale = jnp.exp(jnp.log(0.3) + jax.random.uniform(key_row, (TOKEN_SLOTS, 1)) * jnp.log(10.0))
    values = jnp.clip(jax.random.normal(key_val, (TOKEN_SLOTS, MODEL_WIDTH)), -6.0, 6.0)
    return jnp.clip(values * row_scale, -20.0, 20.0).astype(jnp.bfloat16)


def shard_levels(key, shape, cuts, low, largest):
    gain, own = 1.0, jax.random.fold_in(key, 6)
    for position, parts in cuts:
        draws = jnp.exp(jax.random.uniform(jax.random.fold_in(own, position), (parts,), jnp.float32, low / len(cuts), largest / len(cuts)))
        gain = gain * jnp.repeat(draws, shape[position] // parts).reshape([-1 if axis == position else 1 for axis in range(len(shape))])
    return gain


def normal_values(rng, shape, scale, reach, split=(), kind=jnp.bfloat16):
    level = shard_levels(rng, shape, split, -0.22, 0.18) if split else 1.0
    values = jax.random.normal(rng, shape, jnp.float32) * scale * level
    return jnp.minimum(jnp.maximum(values, -reach), reach).astype(kind)


def setup_inputs(seed: int = 0) -> dict:
    key_of = jax.random.split(jax.random.key(seed), 12)
    return {
        "residual": draw_residual(jax.random.fold_in(key_of[11], 71), 0),
        "query_rows": normal_values(key_of[1], (TOKEN_SLOTS, MODEL_WIDTH), 1.0, 6.0, ((0, 8), (1, 4))),
        "value_rows": normal_values(key_of[2], (TOKEN_SLOTS, MODEL_WIDTH), 1.0, 6.0, ((0, 8), (1, 4))),
        "forget_logit": draw_forget_logit(jax.random.fold_in(key_of[11], 71), 0),
        "slot_kind": draw_slot_kind(jax.random.fold_in(key_of[11], 71), 0),
        "head_gain": jnp.clip(1.0 + 0.18 * jax.random.normal(key_of[5], (MODEL_WIDTH,), jnp.float32), 0.1, 1.9),
        "out_weight": normal_values(key_of[6], (MODEL_WIDTH, MODEL_WIDTH), MODEL_WIDTH ** -0.5, 0.125, ((0, 4), (1, 8))),
        "ffn_gain": jnp.clip(1.0 + 0.18 * jax.random.normal(key_of[7], (MODEL_WIDTH,), jnp.float32), 0.1, 1.9),
        "gate_weight": normal_values(key_of[8], (MODEL_WIDTH, FF), MODEL_WIDTH ** -0.5, 0.125, ((0, 8), (1, 4))),
        "up_weight": normal_values(key_of[9], (MODEL_WIDTH, FF), MODEL_WIDTH ** -0.5, 0.125, ((0, 8), (1, 4))),
        "down_weight": normal_values(key_of[10], (FF, MODEL_WIDTH), FF ** -0.5, 0.109375, ((0, 4), (1, 8))),
    }


def span_step(passed_state, pieces):
    query_block, key_block, value_block, g_block = pieces
    top_precision = lax.Precision.HIGHEST
    inside_block_term = jnp.cumsum(g_block, axis=0)
    between_blocks_term = jnp.einsum('owu,wuj->owj', query_block * jnp.exp(inside_block_term), passed_state, precision=top_precision)
    length = g_block.shape[0]
    causal = jnp.arange(length)[:, None] >= jnp.arange(length)[None, :]
    causal = causal[:, :, None, None]
    gap_log = jnp.where(causal, inside_block_term[:, None] - inside_block_term[None, :], 0.0)
    decay_pairs = jnp.where(causal, jnp.exp(gap_log), 0.0)
    scores = jnp.einsum('tnk,tsnk->tsn', query_block, decay_pairs * key_block[None], precision=top_precision)
    intra_part = jnp.einsum('tsn,snv->tnv', scores, value_block, precision=top_precision)
    final_decay_sum = inside_block_term[-1]
    updated_state = jnp.exp(final_decay_sum)[:, :, None] * passed_state + jnp.einsum('weq,wel->eql', key_block * jnp.exp(final_decay_sum[None] - inside_block_term), value_block, precision=top_precision)
    return (updated_state, between_blocks_term + intra_part)

def reference(residual, query_rows, value_rows, forget_logit, slot_kind, head_gain, out_weight, ffn_gain, gate_weight, up_weight, down_weight):
    live_mask = slot_kind > 0
    first_mask = slot_kind == 2
    log_forget = jnp.where(first_mask[:, None], -80.0, jnp.where(live_mask[:, None], -jax.nn.softplus(-forget_logit), 0.0))
    key_gate = jnp.where(live_mask[:, None], jax.nn.sigmoid(-forget_logit), 0.0)
    shape4 = (TOKEN_SLOTS // SPAN, SPAN, HEADS, HEAD)
    q_all = query_rows.astype(jnp.float32).reshape(shape4)
    v_all = value_rows.astype(jnp.float32).reshape(shape4)
    k_all = key_gate.astype(jnp.float32).reshape(shape4)
    g_all = log_forget.astype(jnp.float32).reshape(shape4)
    start_state = jnp.zeros((HEADS, HEAD, HEAD), jnp.float32)
    _, recurrent = lax.scan(span_step, start_state, (q_all, k_all, v_all, g_all))
    recurrent = recurrent.reshape(TOKEN_SLOTS, HEADS, HEAD)
    mean_sq = lax.optimization_barrier(jnp.mean(recurrent * recurrent, axis=-1, keepdims=True))
    head_normed = (recurrent / jnp.sqrt(mean_sq + 1e-06) * head_gain.reshape(HEADS, HEAD)).astype(jnp.bfloat16)
    head_normed = head_normed.reshape(TOKEN_SLOTS, MODEL_WIDTH)
    group_width = MODEL_WIDTH // N_MLP
    mixed_sum = jnp.zeros((TOKEN_SLOTS, MODEL_WIDTH), jnp.float32)
    for group in range(N_MLP):
        lo_col = group * group_width
        partial_rows = jnp.dot(head_normed[:, lo_col:lo_col + group_width], out_weight[lo_col:lo_col + group_width], preferred_element_type=jnp.float32).astype(jnp.bfloat16)
        mixed_sum = mixed_sum + lax.optimization_barrier(partial_rows).astype(jnp.float32)
    stream = (residual.astype(jnp.float32) + mixed_sum).astype(jnp.bfloat16)

    def ffn_block(inputs):
        stream_rows, live_rows = inputs
        rows_f = stream_rows.astype(jnp.float32)
        ffn_in = (rows_f / jnp.sqrt(lax.optimization_barrier(jnp.mean(rows_f * rows_f, axis=-1, keepdims=True)) + 1e-05) * ffn_gain).astype(jnp.bfloat16)
        gate_acc = jnp.dot(ffn_in, gate_weight, preferred_element_type=jnp.float32)
        up_acc = jnp.dot(ffn_in, up_weight, preferred_element_type=jnp.float32)
        hidden = (jax.nn.silu(gate_acc) * up_acc).astype(jnp.bfloat16)
        ffn_out = jnp.dot(hidden, down_weight, preferred_element_type=jnp.float32)
        result = (rows_f + ffn_out).astype(jnp.bfloat16)
        return jnp.where(live_rows[:, None], result, jnp.zeros_like(result))
    blocks = TOKEN_SLOTS // SLOTS
    layer_out = lax.map(ffn_block, (stream.reshape(blocks, SLOTS, MODEL_WIDTH), live_mask.reshape(blocks, SLOTS)))
    return layer_out.reshape(TOKEN_SLOTS, MODEL_WIDTH)
```

```python
import jax
import jax.numpy as jnp
from jax import lax
from jax.experimental import pallas as pl
from jax.experimental.pallas import tpu as pltpu
from jax.sharding import PartitionSpec as P

HEAD = 128
SPAN = 32


def carried_in(part, axis, combine, identity):
    place = lax.axis_index(axis)
    gathered = jax.tree.map(lambda a: lax.all_gather(a, axis), part)
    state = jax.tree.map(lambda a, e: jnp.zeros_like(a) + jnp.asarray(e, a.dtype), part, identity)

    def one(hop, state):
        return combine(
            state, jax.tree.map(lambda a: lax.dynamic_index_in_dim(a, hop, 0, False), gathered)
        )

    return lax.fori_loop(0, place, one, state)


def span_step(passed_state, pieces):
    query_block, key_block, value_block, g_block = pieces
    top_precision = lax.Precision.HIGHEST
    inside_block_term = jnp.cumsum(g_block, axis=0)
    between_blocks_term = jnp.einsum(
        "owu,wuj->owj",
        query_block * jnp.exp(inside_block_term),
        passed_state,
        precision=top_precision,
    )
    length = g_block.shape[0]
    causal = jnp.arange(length)[:, None] >= jnp.arange(length)[None, :]
    causal = causal[:, :, None, None]
    gap_log = jnp.where(causal, inside_block_term[:, None] - inside_block_term[None, :], 0.0)
    decay_pairs = jnp.where(causal, jnp.exp(gap_log), 0.0)
    scores = jnp.einsum(
        "tnk,tsnk->tsn", query_block, decay_pairs * key_block[None], precision=top_precision
    )
    intra_part = jnp.einsum("tsn,snv->tnv", scores, value_block, precision=top_precision)
    final_decay_sum = inside_block_term[-1]
    updated_state = jnp.exp(final_decay_sum)[:, :, None] * passed_state + jnp.einsum(
        "weq,wel->eql",
        key_block * jnp.exp(final_decay_sum[None] - inside_block_term),
        value_block,
        precision=top_precision,
    )
    return (updated_state, between_blocks_term + intra_part)


def compose(earlier, later):
    return (
        earlier[0] * later[0],
        later[0][:, :, None] * earlier[1] + later[1],
        earlier[2] + later[2],
    )


def on_device(
    residual,
    query_rows,
    value_rows,
    forget_logit,
    slot_kind,
    head_gain,
    out_weight,
    ffn_gain,
    gate_weight,
    up_weight,
    down_weight,
):
    slot_total = residual.shape[0]
    quarter = query_rows.shape[1]
    heads_here = quarter // HEAD
    live_mask = slot_kind > 0
    first_mask = slot_kind == 2
    log_forget = jnp.where(
        first_mask[:, None],
        -80.0,
        jnp.where(live_mask[:, None], -jax.nn.softplus(-forget_logit), 0.0),
    )
    key_gate = jnp.where(live_mask[:, None], jax.nn.sigmoid(-forget_logit), 0.0)
    shape4 = (slot_total // SPAN, SPAN, heads_here, HEAD)
    q_all = query_rows.astype(jnp.float32).reshape(shape4)
    v_all = value_rows.astype(jnp.float32).reshape(shape4)
    k_all = key_gate.reshape(shape4)
    g_all = log_forget.reshape(shape4)
    zero_state = jnp.zeros((heads_here, HEAD, HEAD), jnp.float32)
    decay_whole = jnp.exp(jnp.sum(log_forget, axis=0)).reshape(heads_here, HEAD)
    live_count = jnp.sum(live_mask.astype(jnp.float32))
    neutral = (jnp.ones_like(decay_whole), jnp.zeros_like(zero_state), jnp.zeros((), jnp.float32))
    end_state, local_out = lax.scan(span_step, zero_state, (q_all, k_all, v_all, g_all))
    leading_decay = carried_in((decay_whole, end_state, live_count), "req", compose, neutral)
    within_all = jnp.cumsum(g_all, axis=1)
    block_total = within_all[:, -1]
    blocks = block_total.shape[0]
    earlier = (jnp.arange(blocks)[:, None] > jnp.arange(blocks)[None, :]).astype(jnp.float32)
    before_block = jnp.einsum(
        "mb,bnk->mnk", earlier, block_total, precision=lax.Precision.HIGHEST
    )
    query_damped = q_all * jnp.exp(within_all + before_block[:, None])
    heads_out = local_out + jnp.einsum(
        "mosf,sfl->mosl", query_damped, leading_decay[1], precision=lax.Precision.HIGHEST
    )
    heads_out = heads_out.reshape(slot_total, heads_here, HEAD)
    mean_sq = jnp.mean(heads_out * heads_out, axis=-1, keepdims=True)
    head_normed = (
        heads_out / jnp.sqrt(mean_sq + 1e-06) * head_gain.reshape(heads_here, HEAD)
    ).astype(jnp.bfloat16)
    head_normed = head_normed.reshape(slot_total, quarter)
    partial_rows = jnp.dot(
        head_normed,
        lax.all_gather(out_weight, "req", axis=1, tiled=True),
        preferred_element_type=jnp.float32,
    )
    mixed_sum = lax.psum(partial_rows.astype(jnp.bfloat16), "mlp").astype(jnp.float32)
    stream = (residual.astype(jnp.float32) + mixed_sum).astype(jnp.bfloat16)
    my_cols = lax.axis_index("mlp") * quarter
    rows_f = stream.astype(jnp.float32)
    ffn_in = (
        rows_f / jnp.sqrt(jnp.mean(rows_f * rows_f, axis=-1, keepdims=True) + 1e-05) * ffn_gain
    ).astype(jnp.bfloat16)
    gate_acc = jnp.dot(
        ffn_in,
        lax.all_gather(gate_weight, "req", axis=0, tiled=True),
        preferred_element_type=jnp.float32,
    )
    up_acc = jnp.dot(
        ffn_in,
        lax.all_gather(up_weight, "req", axis=0, tiled=True),
        preferred_element_type=jnp.float32,
    )
    hidden = (jax.nn.silu(gate_acc) * up_acc).astype(jnp.bfloat16)
    terms = jnp.dot(
        hidden,
        lax.all_gather(down_weight, "req", axis=1, tiled=True),
        preferred_element_type=jnp.float32,
    )
    ffn_out = lax.psum_scatter(
        terms.astype(jnp.bfloat16), "mlp", scatter_dimension=1, tiled=True
    ).astype(jnp.float32)
    own_cols = lax.dynamic_slice_in_dim(stream, my_cols, quarter, 1).astype(jnp.float32)
    result = (own_cols + ffn_out).astype(jnp.bfloat16)
    layer_out = jnp.where(live_mask[:, None], result, jnp.zeros_like(result))
    return layer_out


CHUNK = 64
LINE = 4
PAIR = 2
GROUPS = 4
MESH = pl.DeviceIdType.MESH
NT = (((1,), (1,)), ((), ()))
TN = (((0,), (0,)), ((), ()))
NN = (((1,), (0,)), ((), ()))


def mm(a, b, dims=NN):
    return lax.dot_general(a, b, dims, preferred_element_type=jnp.float32)


def layer_kernel(
    residual_far, query_hbm, value_hbm, logit_hbm, kind_row, head_gain, ffn_gain,
    w_out, w_gate, w_up, w_down,
    out,
    residual, query, value, logit, alive,
    g_out, g_gate, g_up, g_down,
    heads_sum, query_far, state, state_out, state_in, decay_out, decay_in,
    normed, part, part_in, stream, ffn_in, hidden, term, term_in,
    load_sem, own_sem, send_sem, recv_sem, st_send, st_recv, dc_send, dc_recv, mx_send, mx_recv,
):
    f32, bf16 = jnp.float32, jnp.bfloat16
    me = lax.axis_index("req")
    grp = lax.axis_index("mlp")
    n_req = LINE * PAIR
    z = me // PAIR
    y = me % PAIR
    mate = me + 1 - 2 * y
    slots, quarter = query.shape
    heads = quarter // HEAD
    own = (w_out, w_gate, w_up, w_down)
    held = (g_out, g_gate, g_up, g_down)
    pieces = range(4)

    loads = [
        pltpu.make_async_copy(src, dst, load_sem.at[i])
        for i, (src, dst) in enumerate(
            ((logit_hbm, logit), (query_hbm, query), (value_hbm, value), (residual_far, residual))
        )
    ]
    keeps = [
        pltpu.make_async_copy(own[p], held[p].at[me], own_sem.at[p]) for p in pieces
    ]
    for copy in loads + keeps:
        copy.start()

    barrier = pltpu.get_barrier_semaphore()
    for d in range(1, n_req):
        pl.semaphore_signal(barrier, inc=1, device_id={"req": (me + d) % n_req}, device_id_type=MESH)
    for d in range(1, GROUPS):
        pl.semaphore_signal(barrier, inc=1, device_id={"mlp": (grp + d) % GROUPS}, device_id_type=MESH)
    pl.semaphore_wait(barrier, n_req - 1 + GROUPS - 1)

    def hop(p, slot, way, src=None):
        target = (mate, me + PAIR, me - PAIR)[way]
        return pltpu.make_async_remote_copy(
            src_ref=held[p].at[slot] if src is None else src,
            dst_ref=held[p].at[slot],
            send_sem=send_sem.at[p, slot, way],
            recv_sem=recv_sem.at[p, slot],
            device_id={"req": target},
            device_id_type=MESH,
        )

    def landed(p, slot):
        hop(p, slot, 0).wait_recv()

    def send_own(p):
        @pl.when(z < LINE - 1)
        def _():
            hop(p, me, 1, own[p]).start()

        @pl.when(z > 0)
        def _():
            hop(p, me, 2, own[p]).start()

        hop(p, me, 0, own[p]).start()

    def relay(p, slot, way):
        landed(p, slot)

        @pl.when(z < LINE - 1 if way == 1 else z > 0)
        def _():
            hop(p, slot, way).start()

        if p > 0:
            hop(p, slot, 0).start()

    def forward(p, k):
        if k == 0:
            landed(0, mate)

            @pl.when(z < LINE - 1)
            def _():
                hop(0, mate, 1).start()

            @pl.when(z > 0)
            def _():
                hop(0, mate, 2).start()

            return

        @pl.when(z >= k)
        def _():
            relay(p, me - PAIR * k, 1)
            if p == 0:
                relay(p, mate - PAIR * k, 1)

        @pl.when(z + k < LINE)
        def _():
            relay(p, me + PAIR * k, 2)
            if p == 0:
                relay(p, mate + PAIR * k, 2)

    def complete(p):
        for j in range(LINE):
            landed(p, PAIR * j + 1 - y)

    for p in (0, 1, 2):
        send_own(p)

    state[...] = jnp.zeros_like(state)
    rows_i = lax.broadcasted_iota(jnp.int32, (CHUNK, CHUNK), 0)
    cols_i = lax.broadcasted_iota(jnp.int32, (CHUNK, CHUNK), 1)
    lower = jnp.where(rows_i >= cols_i, 1.0, 0.0).astype(f32)
    upper = jnp.where(rows_i <= cols_i, 1.0, 0.0).astype(f32)
    ones = jnp.ones((CHUNK, CHUNK), bf16)
    before = jnp.zeros((1, quarter), f32)
    same = jnp.where(rows_i == cols_i, 1.0, 0.0).astype(f32)
    across = jnp.ones((CHUNK, quarter), bf16)
    for copy in loads[:3]:
        copy.wait()
    for c in range(slots // CHUNK):
        rows = pl.ds(c * CHUNK, CHUNK)
        kinds = mm((same * kind_row[c : c + 1, :].astype(f32)).astype(bf16), across)
        live = kinds > 0.5
        alive[rows, :] = kinds
        first_c = jnp.where(kinds[:, :CHUNK] > 1.5, 1.0, 0.0).astype(f32)
        first_r = jnp.where(kind_row[c : c + 1, :] == 2, 1.0, 0.0).astype(f32)
        small = jnp.exp(-logit[rows, :])
        plain = live & (kinds < 1.5)
        g = jnp.where(plain, -jnp.log1p(small), 0.0)
        key = jnp.where(live, small / (1.0 + small), 0.0)
        inner = lax.dot_general(lower, g, NN, precision=lax.Precision.HIGHEST, preferred_element_type=f32)
        count_t = mm((lower * first_r).astype(bf16), ones)
        count_s = mm(ones, (upper * first_c).astype(bf16))
        reset = jnp.where(rows_i >= cols_i, jnp.exp(-80.0 * jnp.maximum(count_t - count_s, 0.0)), 0.0)
        whole = inner - 80.0 * count_t[:, 0:1]
        last = whole[CHUNK - 1 : CHUNK, :]
        q = query[rows, :].astype(f32)
        v = value[rows, :]
        q_in = (q * jnp.exp(inner)).astype(bf16)
        k_in = (key * jnp.exp(-inner)).astype(bf16)
        q_old = (q * jnp.exp(whole)).astype(bf16)
        k_end = (key * jnp.exp(last - whole)).astype(bf16)
        query_far[rows, :] = (q * jnp.exp(whole + before)).astype(bf16)
        keep = jnp.exp(last)
        before = before + last
        for h in range(heads):
            cols = slice(h * HEAD, (h + 1) * HEAD)
            scores = (mm(q_in[:, cols], k_in[:, cols], NT) * reset).astype(bf16)
            old = state[:, cols]
            heads_sum[rows, cols] = mm(scores, v[:, cols]) + mm(q_old[:, cols], old.astype(bf16), NT)
            state[:, cols] = keep[:, cols] * old + mm(v[:, cols], k_end[:, cols], TN)
        if c == 0:
            forward(0, 0)
        if c == 1:
            send_own(3)
        if c == 2:
            forward(0, 1)

    state_out[...] = state[...].astype(bf16)
    decay_out[...] = jnp.broadcast_to(jnp.exp(before), decay_out.shape)

    def to_later(d, slot, target):
        return (
            pltpu.make_async_remote_copy(
                src_ref=state_out, dst_ref=state_in.at[slot], send_sem=st_send.at[d],
                recv_sem=st_recv.at[slot], device_id={"req": target}, device_id_type=MESH,
            ),
            pltpu.make_async_remote_copy(
                src_ref=decay_out, dst_ref=decay_in.at[slot], send_sem=dc_send.at[d],
                recv_sem=dc_recv.at[slot], device_id={"req": target}, device_id_type=MESH,
            ),
        )

    for d in range(1, n_req):
        @pl.when(me + d < n_req)
        def _(d=d):
            for copy in to_later(d, me, me + d):
                copy.start()

    forward(1, 1)
    forward(2, 1)
    forward(0, 2)
    forward(3, 1)

    state[...] = jnp.zeros_like(state)

    def carry(u, _):
        for copy in to_later(0, u, mate):
            copy.wait_recv()
        state[...] = decay_in[u][0:1, :] * state[...] + state_in[u].astype(f32)
        return 0

    lax.fori_loop(0, me, carry, 0)
    forward(0, 3)
    for h in range(heads):
        cols = slice(h * HEAD, (h + 1) * HEAD)
        o = heads_sum[:, cols] + mm(query_far[:, cols], state[:, cols].astype(bf16), NT)
        mean_sq = jnp.mean(o * o, axis=-1, keepdims=True)
        normed[:, cols] = (o / jnp.sqrt(mean_sq + 1e-06) * head_gain[:, cols]).astype(bf16)
    forward(1, 2)
    forward(2, 2)
    for copy in keeps + loads[3:]:
        copy.wait()

    wide = w_out.shape[1]
    per = n_req // GROUPS
    for r in range(n_req):
        at = slice((r % per) * wide, (r % per + 1) * wide)
        part[r // per, :, at] = mm(normed[...], g_out[r]).astype(bf16)

    def to_group(step, src, dst, slot, target):
        return pltpu.make_async_remote_copy(
            src_ref=src, dst_ref=dst, send_sem=mx_send.at[step, target],
            recv_sem=mx_recv.at[step, slot], device_id={"mlp": target}, device_id_type=MESH,
        )

    def exchange(step, source, into):
        copies = []
        for d in range(1, GROUPS):
            other = (grp + d) % GROUPS
            copy = to_group(step, source(other), into.at[grp], d, other)
            copy.start()
            copies.append(copy)
        return copies

    first = exchange(0, lambda j: part.at[j], part_in)
    forward(3, 2)
    my_part = part[grp].astype(f32)
    for copy in first:
        copy.wait_recv()
    total = my_part
    for d in range(1, GROUPS):
        total = total + part_in[(grp + d) % GROUPS].astype(f32)
    mine = residual[:, pl.ds(pl.multiple_of(grp * quarter, quarter), quarter)]
    stream[grp] = (mine.astype(f32) + total).astype(bf16)
    second = exchange(1, lambda j: stream.at[grp], stream)
    forward(1, 3)
    forward(2, 3)
    for copy in second:
        copy.wait_recv()
    square = jnp.zeros((slots, 1), f32)
    for j in range(GROUPS):
        s = stream[j].astype(f32)
        square = square + jnp.sum(s * s, axis=-1, keepdims=True)
    width = quarter * GROUPS
    scale = jnp.sqrt(square / width + 1e-05)
    for j in range(GROUPS):
        ffn_in[j] = (stream[j].astype(f32) / scale * ffn_gain[j : j + 1, :]).astype(bf16)
    complete(1)
    complete(2)
    deep = w_gate.shape[0]
    gate = jnp.zeros((slots, w_gate.shape[1]), f32)
    up = jnp.zeros((slots, w_gate.shape[1]), f32)
    for r in range(n_req):
        x = ffn_in[r // per, :, (r % per) * deep : (r % per + 1) * deep]
        gate = gate + mm(x, g_gate[r])
        up = up + mm(x, g_up[r])
    hidden[...] = (gate / (1.0 + jnp.exp(-gate)) * up).astype(bf16)

    def down(j):
        landed(3, PAIR * j + 1 - y)
        for i in range(PAIR):
            at = slice(i * wide, (i + 1) * wide)
            term[j, :, at] = mm(hidden[...], g_down[PAIR * j + i]).astype(bf16)

        @pl.when(grp != j)
        def _():
            to_group(2, term.at[j], term_in.at[grp], grp, j).start()

    down(z)
    for k in range(1, LINE):
        if k == LINE - 1:
            forward(3, k)

        @pl.when(z >= k)
        def _(k=k):
            down(z - k)

        @pl.when(z + k < LINE)
        def _(k=k):
            down(z + k)

    total = term[grp].astype(f32)
    for d in range(1, GROUPS):
        other = (grp + d) % GROUPS
        to_group(2, term.at[other], term_in.at[other], other, other).wait_recv()
        total = total + term_in[other].astype(f32)
    result = (stream[grp].astype(f32) + total).astype(bf16)
    out[...] = jnp.where(alive[...] > 0.5, result, jnp.zeros_like(result))

    for copy in first + second:
        copy.wait_send()
    for d in range(1, GROUPS):
        other = (grp + d) % GROUPS
        to_group(2, term.at[other], term_in.at[grp], grp, other).wait_send()
    for d in range(1, n_req):
        @pl.when(me + d < n_req)
        def _(d=d):
            for copy in to_later(d, me, me + d):
                copy.wait_send()
    def sent(p, slot, up, down, over):
        if over:
            hop(p, slot, 0).wait_send()
        if up:
            @pl.when(z < LINE - 1)
            def _():
                hop(p, slot, 1).wait_send()
        if down:
            @pl.when(z > 0)
            def _():
                hop(p, slot, 2).wait_send()

    for p in pieces:
        sent(p, me, True, True, True)
        if p == 0:
            sent(p, mate, True, True, False)
        for k in range(1, LINE):
            @pl.when(z >= k)
            def _(p=p, k=k):
                sent(p, me - PAIR * k, True, False, p > 0)
                if p == 0:
                    sent(p, mate - PAIR * k, True, False, False)

            @pl.when(z + k < LINE)
            def _(p=p, k=k):
                sent(p, me + PAIR * k, False, True, p > 0)
                if p == 0:
                    sent(p, mate + PAIR * k, False, True, False)


def in_one_kernel(
    residual, query_rows, value_rows, forget_logit, slot_kind, head_gain,
    out_weight, ffn_gain, gate_weight, up_weight, down_weight,
):
    f32, bf16 = jnp.float32, jnp.bfloat16
    slots, quarter = query_rows.shape
    n_req = LINE * PAIR
    dma = pltpu.SemaphoreType.DMA
    vmem = pltpu.VMEM
    cube = (GROUPS, slots, quarter)
    return pl.pallas_call(
        layer_kernel,
        out_shape=jax.ShapeDtypeStruct((slots, quarter), bf16),
        in_specs=[pl.BlockSpec(memory_space=pltpu.HBM)] * 4
        + [pl.BlockSpec(memory_space=pltpu.VMEM)] * 3
        + [pl.BlockSpec(memory_space=pltpu.HBM)] * 4,
        out_specs=pl.BlockSpec(memory_space=pltpu.VMEM),
        scratch_shapes=[
            vmem(residual.shape, bf16),
            vmem((slots, quarter), bf16),
            vmem((slots, quarter), bf16),
            vmem((slots, quarter), f32),
            vmem((slots, quarter), f32),
            vmem((n_req, *out_weight.shape), bf16),
            vmem((n_req, *gate_weight.shape), bf16),
            vmem((n_req, *up_weight.shape), bf16),
            vmem((n_req, *down_weight.shape), bf16),
            vmem((slots, quarter), f32),
            vmem((slots, quarter), bf16),
            vmem((HEAD, quarter), f32),
            vmem((HEAD, quarter), bf16),
            vmem((n_req, HEAD, quarter), bf16),
            vmem((8, quarter), f32),
            vmem((n_req, 8, quarter), f32),
            vmem((slots, quarter), bf16),
            vmem(cube, bf16),
            vmem(cube, bf16),
            vmem(cube, bf16),
            vmem(cube, bf16),
            vmem((slots, gate_weight.shape[1]), bf16),
            vmem(cube, bf16),
            vmem(cube, bf16),
            dma((4,)),
            dma((4,)),
            dma((4, n_req, 3)),
            dma((4, n_req)),
            dma((n_req,)),
            dma((n_req,)),
            dma((n_req,)),
            dma((n_req,)),
            dma((3, GROUPS)),
            dma((3, GROUPS)),
        ],
        compiler_params=pltpu.CompilerParams(
            collective_id=0, has_side_effects=True, vmem_limit_bytes=50 << 20
        ),
        cost_estimate=pl.CostEstimate(flops=6 << 30, bytes_accessed=16 << 20, transcendentals=1 << 20),
    )(
        residual,
        query_rows, value_rows, forget_logit,
        slot_kind.reshape(slots // CHUNK, CHUNK),
        head_gain.reshape(1, quarter), ffn_gain.reshape(GROUPS, quarter),
        out_weight, gate_weight, up_weight, down_weight,
    )


def solution(mesh):
    fits = mesh.shape["req"] == LINE * PAIR and mesh.shape["mlp"] == GROUPS
    return jax.shard_map(
        in_one_kernel if fits else on_device,
        mesh=mesh,
        in_specs=(
            P("req", None),
            P("req", "mlp"),
            P("req", "mlp"),
            P("req", "mlp"),
            P("req"),
            P("mlp"),
            P("mlp", "req"),
            P(),
            P("req", "mlp"),
            P("req", "mlp"),
            P("mlp", "req"),
        ),
        out_specs=P("req", "mlp"),
        check_vma=False,
    )
```

```python
import jax
import jax.numpy as jnp
from jax import lax
from jax.experimental import pallas as pl
from jax.experimental.pallas import tpu as pltpu
from jax.sharding import PartitionSpec as P

HEAD = 128
SPAN = 32


def carried_in(part, axis, combine, identity):
    place = lax.axis_index(axis)
    gathered = jax.tree.map(lambda a: lax.all_gather(a, axis), part)
    state = jax.tree.map(lambda a, e: jnp.zeros_like(a) + jnp.asarray(e, a.dtype), part, identity)

    def one(hop, state):
        return combine(
            state, jax.tree.map(lambda a: lax.dynamic_index_in_dim(a, hop, 0, False), gathered)
        )

    return lax.fori_loop(0, place, one, state)


def span_step(passed_state, pieces):
    query_block, key_block, value_block, g_block = pieces
    top_precision = lax.Precision.HIGHEST
    inside_block_term = jnp.cumsum(g_block, axis=0)
    between_blocks_term = jnp.einsum(
        "owu,wuj->owj",
        query_block * jnp.exp(inside_block_term),
        passed_state,
        precision=top_precision,
    )
    length = g_block.shape[0]
    causal = jnp.arange(length)[:, None] >= jnp.arange(length)[None, :]
    causal = causal[:, :, None, None]
    gap_log = jnp.where(causal, inside_block_term[:, None] - inside_block_term[None, :], 0.0)
    decay_pairs = jnp.where(causal, jnp.exp(gap_log), 0.0)
    scores = jnp.einsum(
        "tnk,tsnk->tsn", query_block, decay_pairs * key_block[None], precision=top_precision
    )
    intra_part = jnp.einsum("tsn,snv->tnv", scores, value_block, precision=top_precision)
    final_decay_sum = inside_block_term[-1]
    updated_state = jnp.exp(final_decay_sum)[:, :, None] * passed_state + jnp.einsum(
        "weq,wel->eql",
        key_block * jnp.exp(final_decay_sum[None] - inside_block_term),
        value_block,
        precision=top_precision,
    )
    return (updated_state, between_blocks_term + intra_part)


def compose(earlier, later):
    return (
        earlier[0] * later[0],
        later[0][:, :, None] * earlier[1] + later[1],
        earlier[2] + later[2],
    )


def on_device(
    residual,
    query_rows,
    value_rows,
    forget_logit,
    slot_kind,
    head_gain,
    out_weight,
    ffn_gain,
    gate_weight,
    up_weight,
    down_weight,
):
    slot_total = residual.shape[0]
    quarter = query_rows.shape[1]
    heads_here = quarter // HEAD
    live_mask = slot_kind > 0
    first_mask = slot_kind == 2
    log_forget = jnp.where(
        first_mask[:, None],
        -80.0,
        jnp.where(live_mask[:, None], -jax.nn.softplus(-forget_logit), 0.0),
    )
    key_gate = jnp.where(live_mask[:, None], jax.nn.sigmoid(-forget_logit), 0.0)
    shape4 = (slot_total // SPAN, SPAN, heads_here, HEAD)
    q_all = query_rows.astype(jnp.float32).reshape(shape4)
    v_all = value_rows.astype(jnp.float32).reshape(shape4)
    k_all = key_gate.reshape(shape4)
    g_all = log_forget.reshape(shape4)
    zero_state = jnp.zeros((heads_here, HEAD, HEAD), jnp.float32)
    decay_whole = jnp.exp(jnp.sum(log_forget, axis=0)).reshape(heads_here, HEAD)
    live_count = jnp.sum(live_mask.astype(jnp.float32))
    neutral = (jnp.ones_like(decay_whole), jnp.zeros_like(zero_state), jnp.zeros((), jnp.float32))
    end_state, local_out = lax.scan(span_step, zero_state, (q_all, k_all, v_all, g_all))
    leading_decay = carried_in((decay_whole, end_state, live_count), "req", compose, neutral)
    within_all = jnp.cumsum(g_all, axis=1)
    block_total = within_all[:, -1]
    blocks = block_total.shape[0]
    earlier = (jnp.arange(blocks)[:, None] > jnp.arange(blocks)[None, :]).astype(jnp.float32)
    before_block = jnp.einsum(
        "mb,bnk->mnk", earlier, block_total, precision=lax.Precision.HIGHEST
    )
    query_damped = q_all * jnp.exp(within_all + before_block[:, None])
    heads_out = local_out + jnp.einsum(
        "mosf,sfl->mosl", query_damped, leading_decay[1], precision=lax.Precision.HIGHEST
    )
    heads_out = heads_out.reshape(slot_total, heads_here, HEAD)
    mean_sq = jnp.mean(heads_out * heads_out, axis=-1, keepdims=True)
    head_normed = (
        heads_out / jnp.sqrt(mean_sq + 1e-06) * head_gain.reshape(heads_here, HEAD)
    ).astype(jnp.bfloat16)
    head_normed = head_normed.reshape(slot_total, quarter)
    partial_rows = jnp.dot(
        head_normed,
        lax.all_gather(out_weight, "req", axis=1, tiled=True),
        preferred_element_type=jnp.float32,
    )
    mixed_sum = lax.psum(partial_rows.astype(jnp.bfloat16), "mlp").astype(jnp.float32)
    stream = (residual.astype(jnp.float32) + mixed_sum).astype(jnp.bfloat16)
    my_cols = lax.axis_index("mlp") * quarter
    rows_f = stream.astype(jnp.float32)
    ffn_in = (
        rows_f / jnp.sqrt(jnp.mean(rows_f * rows_f, axis=-1, keepdims=True) + 1e-05) * ffn_gain
    ).astype(jnp.bfloat16)
    gate_acc = jnp.dot(
        ffn_in,
        lax.all_gather(gate_weight, "req", axis=0, tiled=True),
        preferred_element_type=jnp.float32,
    )
    up_acc = jnp.dot(
        ffn_in,
        lax.all_gather(up_weight, "req", axis=0, tiled=True),
        preferred_element_type=jnp.float32,
    )
    hidden = (jax.nn.silu(gate_acc) * up_acc).astype(jnp.bfloat16)
    terms = jnp.dot(
        hidden,
        lax.all_gather(down_weight, "req", axis=1, tiled=True),
        preferred_element_type=jnp.float32,
    )
    ffn_out = lax.psum_scatter(
        terms.astype(jnp.bfloat16), "mlp", scatter_dimension=1, tiled=True
    ).astype(jnp.float32)
    own_cols = lax.dynamic_slice_in_dim(stream, my_cols, quarter, 1).astype(jnp.float32)
    result = (own_cols + ffn_out).astype(jnp.bfloat16)
    layer_out = jnp.where(live_mask[:, None], result, jnp.zeros_like(result))
    return layer_out


CHUNK = 64
LINE = 4
PAIR = 2
GROUPS = 4
MESH = pl.DeviceIdType.MESH
NT = (((1,), (1,)), ((), ()))
TN = (((0,), (0,)), ((), ()))
NN = (((1,), (0,)), ((), ()))


def mm(a, b, dims=NN):
    return lax.dot_general(a, b, dims, preferred_element_type=jnp.float32)


def layer_kernel(
    residual_far, query_hbm, value_hbm, logit_hbm, kind_row, head_gain, ffn_gain,
    w_out, w_gate, w_up, w_down,
    out,
    residual, query, value, logit, alive,
    g_out, g_gate, g_up, g_down,
    heads_sum, query_far, state, state_out, state_pair, state_in, decay_out, decay_pair, decay_in,
    normed, part, part_in, stream, ffn_in, hidden, term, term_in,
    load_sem, own_sem, send_sem, recv_sem, st_send, st_recv, dc_send, dc_recv, mx_send, mx_recv,
):
    f32, bf16 = jnp.float32, jnp.bfloat16
    me = lax.axis_index("req")
    grp = lax.axis_index("mlp")
    n_req = LINE * PAIR
    z = me // PAIR
    y = me % PAIR
    mate = me + 1 - 2 * y
    slots, quarter = query.shape
    heads = quarter // HEAD
    half_out, half_down = w_out.shape[0] // 2, w_down.shape[0] // 2
    table = (
        (w_out, g_out, 0, half_out),
        (w_gate, g_gate, 0, w_gate.shape[0]),
        (w_up, g_up, 0, w_up.shape[0]),
        (w_down, g_down, 0, half_down),
        (w_out, g_out, half_out, half_out),
        (w_down, g_down, half_down, half_down),
    )
    pieces = range(len(table))

    def own(p):
        shard, _, start, count = table[p]
        return shard.at[pl.ds(start, count), :]

    def held(p, slot):
        _, gathered, start, count = table[p]
        return gathered.at[slot, pl.ds(start, count), :]


    loads = [
        pltpu.make_async_copy(src, dst, load_sem.at[i])
        for i, (src, dst) in enumerate(
            ((logit_hbm, logit), (query_hbm, query), (value_hbm, value), (residual_far, residual))
        )
    ]
    keeps = [
        pltpu.make_async_copy(own(p), held(p, me), own_sem.at[p]) for p in pieces
    ]
    for copy in loads + keeps:
        copy.start()

    barrier = pltpu.get_barrier_semaphore()
    for d in range(1, n_req):
        pl.semaphore_signal(barrier, inc=1, device_id={"req": (me + d) % n_req}, device_id_type=MESH)
    for d in range(1, GROUPS):
        pl.semaphore_signal(barrier, inc=1, device_id={"mlp": (grp + d) % GROUPS}, device_id_type=MESH)
    pl.semaphore_wait(barrier, n_req - 1 + GROUPS - 1)

    def hop(p, slot, way, src=None):
        target = (mate, me + PAIR, me - PAIR)[way]
        return pltpu.make_async_remote_copy(
            src_ref=held(p, slot) if src is None else src,
            dst_ref=held(p, slot),
            send_sem=send_sem.at[p, slot, way],
            recv_sem=recv_sem.at[p, slot],
            device_id={"req": target},
            device_id_type=MESH,
        )

    def landed(p, slot):
        hop(p, slot, 0).wait_recv()

    def send_own(p):
        @pl.when(z < LINE - 1)
        def _():
            hop(p, me, 1, own(p)).start()

        @pl.when(z > 0)
        def _():
            hop(p, me, 2, own(p)).start()

        hop(p, me, 0, own(p)).start()

    def relay(p, slot, way):
        landed(p, slot)

        @pl.when(z < LINE - 1 if way == 1 else z > 0)
        def _():
            hop(p, slot, way).start()

        if p > 0:
            hop(p, slot, 0).start()

    def forward(p, k):
        if k == 0:
            landed(0, mate)

            @pl.when(z < LINE - 1)
            def _():
                hop(0, mate, 1).start()

            @pl.when(z > 0)
            def _():
                hop(0, mate, 2).start()

            return

        @pl.when(z >= k)
        def _():
            relay(p, me - PAIR * k, 1)
            if p == 0:
                relay(p, mate - PAIR * k, 1)

        @pl.when(z + k < LINE)
        def _():
            relay(p, me + PAIR * k, 2)
            if p == 0:
                relay(p, mate + PAIR * k, 2)

    def complete(p):
        for j in range(LINE):
            landed(p, PAIR * j + 1 - y)

    for p in (0, 4, 1, 2):
        send_own(p)

    state[...] = jnp.zeros_like(state)
    rows_i = lax.broadcasted_iota(jnp.int32, (CHUNK, CHUNK), 0)
    cols_i = lax.broadcasted_iota(jnp.int32, (CHUNK, CHUNK), 1)
    lower = jnp.where(rows_i >= cols_i, 1.0, 0.0).astype(f32)
    upper = jnp.where(rows_i <= cols_i, 1.0, 0.0).astype(f32)
    ones = jnp.ones((CHUNK, CHUNK), bf16)
    before = jnp.zeros((1, quarter), f32)
    same = jnp.where(rows_i == cols_i, 1.0, 0.0).astype(f32)
    across = jnp.ones((CHUNK, quarter), bf16)
    for copy in loads[:3]:
        copy.wait()
    for c in range(slots // CHUNK):
        rows = pl.ds(c * CHUNK, CHUNK)
        kinds = mm((same * kind_row[c : c + 1, :].astype(f32)).astype(bf16), across)
        live = kinds > 0.5
        alive[rows, :] = kinds
        first_c = jnp.where(kinds[:, :CHUNK] > 1.5, 1.0, 0.0).astype(f32)
        first_r = jnp.where(kind_row[c : c + 1, :] == 2, 1.0, 0.0).astype(f32)
        small = jnp.exp(-logit[rows, :])
        plain = live & (kinds < 1.5)
        g = jnp.where(plain, -jnp.log1p(small), 0.0)
        key = jnp.where(live, small / (1.0 + small), 0.0)
        inner = lax.dot_general(lower, g, NN, precision=lax.Precision.HIGHEST, preferred_element_type=f32)
        count_t = mm((lower * first_r).astype(bf16), ones)
        count_s = mm(ones, (upper * first_c).astype(bf16))
        reset = jnp.where(rows_i >= cols_i, jnp.exp(-80.0 * jnp.maximum(count_t - count_s, 0.0)), 0.0)
        whole = inner - 80.0 * count_t[:, 0:1]
        last = whole[CHUNK - 1 : CHUNK, :]
        q = query[rows, :].astype(f32)
        v = value[rows, :]
        q_in = (q * jnp.exp(inner)).astype(bf16)
        k_in = (key * jnp.exp(-inner)).astype(bf16)
        q_old = (q * jnp.exp(whole)).astype(bf16)
        k_end = (key * jnp.exp(last - whole)).astype(bf16)
        query_far[rows, :] = (q * jnp.exp(whole + before)).astype(bf16)
        keep = jnp.exp(last)
        before = before + last
        for h in range(heads):
            cols = slice(h * HEAD, (h + 1) * HEAD)
            scores = (mm(q_in[:, cols], k_in[:, cols], NT) * reset).astype(bf16)
            old = state[:, cols]
            heads_sum[rows, cols] = mm(scores, v[:, cols]) + mm(q_old[:, cols], old.astype(bf16), NT)
            state[:, cols] = keep[:, cols] * old + mm(v[:, cols], k_end[:, cols], TN)
        if c == 0:
            forward(0, 0)
        if c == 1:
            send_own(3)
            send_own(5)
        if c == 2:
            forward(0, 1)
            forward(4, 1)

    state_out[...] = state[...].astype(bf16)
    decay_out[...] = jnp.broadcast_to(jnp.exp(before), decay_out.shape)

    def pass_on(src, decay, d, slot, target):
        return (
            pltpu.make_async_remote_copy(
                src_ref=src, dst_ref=state_in.at[slot], send_sem=st_send.at[d],
                recv_sem=st_recv.at[slot], device_id={"req": target}, device_id_type=MESH,
            ),
            pltpu.make_async_remote_copy(
                src_ref=decay, dst_ref=decay_in.at[slot], send_sem=dc_send.at[d],
                recv_sem=dc_recv.at[slot], device_id={"req": target}, device_id_type=MESH,
            ),
        )

    to_mate = pass_on(state_out, decay_out, 0, LINE, mate)
    for copy in to_mate:
        copy.start()
    forward(1, 1)
    for copy in to_mate:
        copy.wait_recv()
    d_own, s_own = decay_out[...], state[...]
    d_mate, s_mate = decay_in[LINE], state_in[LINE].astype(f32)
    early = y == 0
    state_pair[...] = (
        jnp.where(early, s_own, s_mate) * jnp.where(early, d_mate, d_own)[0:1, :]
        + jnp.where(early, s_mate, s_own)
    ).astype(bf16)
    decay_pair[...] = d_own * d_mate
    for k in range(1, LINE):
        @pl.when(z + k < LINE)
        def _(k=k):
            for copy in pass_on(state_pair, decay_pair, k, z, me + PAIR * k):
                copy.start()

    forward(2, 1)
    forward(0, 2)
    forward(4, 2)
    forward(3, 1)
    forward(5, 1)
    forward(1, 2)
    forward(2, 2)

    state[...] = jnp.zeros_like(state)

    def carry(u, _):
        for copy in pass_on(state_pair, decay_pair, 0, u, mate):
            copy.wait_recv()
        state[...] = decay_in[u][0:1, :] * state[...] + state_in[u].astype(f32)
        return 0

    lax.fori_loop(0, z, carry, 0)

    @pl.when(y == 1)
    def _():
        state[...] = decay_in[LINE][0:1, :] * state[...] + state_in[LINE].astype(f32)

    forward(0, 3)
    forward(4, 3)
    for h in range(heads):
        cols = slice(h * HEAD, (h + 1) * HEAD)
        o = heads_sum[:, cols] + mm(query_far[:, cols], state[:, cols].astype(bf16), NT)
        mean_sq = jnp.mean(o * o, axis=-1, keepdims=True)
        normed[:, cols] = (o / jnp.sqrt(mean_sq + 1e-06) * head_gain[:, cols]).astype(bf16)
    complete(4)
    for copy in keeps + loads[3:]:
        copy.wait()

    wide = w_out.shape[1]
    per = n_req // GROUPS
    for r in range(n_req):
        at = slice((r % per) * wide, (r % per + 1) * wide)
        part[r // per, :, at] = mm(normed[...], g_out[r]).astype(bf16)

    def to_group(step, src, dst, slot, target):
        return pltpu.make_async_remote_copy(
            src_ref=src, dst_ref=dst, send_sem=mx_send.at[step, target],
            recv_sem=mx_recv.at[step, slot], device_id={"mlp": target}, device_id_type=MESH,
        )

    def exchange(step, source, into):
        copies = []
        for d in range(1, GROUPS):
            other = (grp + d) % GROUPS
            copy = to_group(step, source(other), into.at[grp], d, other)
            copy.start()
            copies.append(copy)
        return copies

    first = exchange(0, lambda j: part.at[j], part_in)
    forward(3, 2)
    forward(5, 2)
    my_part = part[grp].astype(f32)
    for copy in first:
        copy.wait_recv()
    total = my_part
    for d in range(1, GROUPS):
        total = total + part_in[(grp + d) % GROUPS].astype(f32)
    mine = residual[:, pl.ds(pl.multiple_of(grp * quarter, quarter), quarter)]
    stream[grp] = (mine.astype(f32) + total).astype(bf16)
    second = exchange(1, lambda j: stream.at[grp], stream)
    forward(1, 3)
    forward(2, 3)
    for copy in second:
        copy.wait_recv()
    square = jnp.zeros((slots, 1), f32)
    for j in range(GROUPS):
        s = stream[j].astype(f32)
        square = square + jnp.sum(s * s, axis=-1, keepdims=True)
    width = quarter * GROUPS
    scale = jnp.sqrt(square / width + 1e-05)
    for j in range(GROUPS):
        ffn_in[j] = (stream[j].astype(f32) / scale * ffn_gain[j : j + 1, :]).astype(bf16)
    complete(1)
    complete(2)
    deep = w_gate.shape[0]
    gate = jnp.zeros((slots, w_gate.shape[1]), f32)
    up = jnp.zeros((slots, w_gate.shape[1]), f32)
    for r in range(n_req):
        x = ffn_in[r // per, :, (r % per) * deep : (r % per + 1) * deep]
        gate = gate + mm(x, g_gate[r])
        up = up + mm(x, g_up[r])
    hidden[...] = (gate / (1.0 + jnp.exp(-gate)) * up).astype(bf16)

    def down(j):
        landed(3, PAIR * j + 1 - y)
        landed(5, PAIR * j + 1 - y)
        for i in range(PAIR):
            at = slice(i * wide, (i + 1) * wide)
            term[j, :, at] = mm(hidden[...], g_down[PAIR * j + i]).astype(bf16)

        @pl.when(grp != j)
        def _():
            to_group(2, term.at[j], term_in.at[grp], grp, j).start()

    down(z)
    for k in range(1, LINE):
        if k == LINE - 1:
            forward(3, k)
            forward(5, k)

        @pl.when(z >= k)
        def _(k=k):
            down(z - k)

        @pl.when(z + k < LINE)
        def _(k=k):
            down(z + k)

    total = term[grp].astype(f32)
    for d in range(1, GROUPS):
        other = (grp + d) % GROUPS
        to_group(2, term.at[other], term_in.at[other], other, other).wait_recv()
        total = total + term_in[other].astype(f32)
    result = (stream[grp].astype(f32) + total).astype(bf16)
    out[...] = jnp.where(alive[...] > 0.5, result, jnp.zeros_like(result))

    for copy in first + second:
        copy.wait_send()
    for d in range(1, GROUPS):
        other = (grp + d) % GROUPS
        to_group(2, term.at[other], term_in.at[grp], grp, other).wait_send()
    for copy in to_mate:
        copy.wait_send()
    for k in range(1, LINE):
        @pl.when(z + k < LINE)
        def _(k=k):
            for copy in pass_on(state_pair, decay_pair, k, z, me + PAIR * k):
                copy.wait_send()
    def sent(p, slot, up, down, over):
        if over:
            hop(p, slot, 0).wait_send()
        if up:
            @pl.when(z < LINE - 1)
            def _():
                hop(p, slot, 1).wait_send()
        if down:
            @pl.when(z > 0)
            def _():
                hop(p, slot, 2).wait_send()

    for p in pieces:
        sent(p, me, True, True, True)
        if p == 0:
            sent(p, mate, True, True, False)
        for k in range(1, LINE):
            @pl.when(z >= k)
            def _(p=p, k=k):
                sent(p, me - PAIR * k, True, False, p > 0)
                if p == 0:
                    sent(p, mate - PAIR * k, True, False, False)

            @pl.when(z + k < LINE)
            def _(p=p, k=k):
                sent(p, me + PAIR * k, False, True, p > 0)
                if p == 0:
                    sent(p, mate + PAIR * k, False, True, False)


def in_one_kernel(
    residual, query_rows, value_rows, forget_logit, slot_kind, head_gain,
    out_weight, ffn_gain, gate_weight, up_weight, down_weight,
):
    f32, bf16 = jnp.float32, jnp.bfloat16
    slots, quarter = query_rows.shape
    n_req = LINE * PAIR
    dma = pltpu.SemaphoreType.DMA
    vmem = pltpu.VMEM
    cube = (GROUPS, slots, quarter)
    return pl.pallas_call(
        layer_kernel,
        out_shape=jax.ShapeDtypeStruct((slots, quarter), bf16),
        in_specs=[pl.BlockSpec(memory_space=pltpu.HBM)] * 4
        + [pl.BlockSpec(memory_space=pltpu.VMEM)] * 3
        + [pl.BlockSpec(memory_space=pltpu.HBM)] * 4,
        out_specs=pl.BlockSpec(memory_space=pltpu.VMEM),
        scratch_shapes=[
            vmem(residual.shape, bf16),
            vmem((slots, quarter), bf16),
            vmem((slots, quarter), bf16),
            vmem((slots, quarter), f32),
            vmem((slots, quarter), f32),
            vmem((n_req, *out_weight.shape), bf16),
            vmem((n_req, *gate_weight.shape), bf16),
            vmem((n_req, *up_weight.shape), bf16),
            vmem((n_req, *down_weight.shape), bf16),
            vmem((slots, quarter), f32),
            vmem((slots, quarter), bf16),
            vmem((HEAD, quarter), f32),
            vmem((HEAD, quarter), bf16),
            vmem((HEAD, quarter), bf16),
            vmem((LINE + 1, HEAD, quarter), bf16),
            vmem((8, quarter), f32),
            vmem((8, quarter), f32),
            vmem((LINE + 1, 8, quarter), f32),
            vmem((slots, quarter), bf16),
            vmem(cube, bf16),
            vmem(cube, bf16),
            vmem(cube, bf16),
            vmem(cube, bf16),
            vmem((slots, gate_weight.shape[1]), bf16),
            vmem(cube, bf16),
            vmem(cube, bf16),
            dma((4,)),
            dma((6,)),
            dma((6, n_req, 3)),
            dma((6, n_req)),
            dma((LINE,)),
            dma((LINE + 1,)),
            dma((LINE,)),
            dma((LINE + 1,)),
            dma((3, GROUPS)),
            dma((3, GROUPS)),
        ],
        compiler_params=pltpu.CompilerParams(
            collective_id=0, has_side_effects=True, vmem_limit_bytes=60 << 20
        ),
        cost_estimate=pl.CostEstimate(flops=6 << 30, bytes_accessed=16 << 20, transcendentals=1 << 20),
    )(
        residual,
        query_rows, value_rows, forget_logit,
        slot_kind.reshape(slots // CHUNK, CHUNK),
        head_gain.reshape(1, quarter), ffn_gain.reshape(GROUPS, quarter),
        out_weight, gate_weight, up_weight, down_weight,
    )


def solution(mesh):
    fits = mesh.shape["req"] == LINE * PAIR and mesh.shape["mlp"] == GROUPS
    return jax.shard_map(
        in_one_kernel if fits else on_device,
        mesh=mesh,
        in_specs=(
            P("req", None),
            P("req", "mlp"),
            P("req", "mlp"),
            P("req", "mlp"),
            P("req"),
            P("mlp"),
            P("mlp", "req"),
            P(),
            P("req", "mlp"),
            P("req", "mlp"),
            P("mlp", "req"),
        ),
        out_specs=P("req", "mlp"),
        check_vma=False,
    )
```
